128 devices in a mesh: ctx: 32 (over x, z, y_lo), head: 4 (over y_hi, core).
Axes of the slice: x: 4, y: 4 (y_hi: 2, y_lo: 2; y = y_hi * 2 + y_lo), z: 4, core: 2. Of those that a mesh axis runs over, the one named last changes fastest.
Arguments:
- attn_query: bfloat16 [16384, 6144], P('ctx', 'head'), may hold values from -16 to 16
- attn_key: bfloat16 [16384, 6144], P('ctx', 'head'), may hold values from -16 to 16
- attn_value: bfloat16 [16384, 6144], P('ctx', 'head'), may hold values from -120 to 120
- delta_query: bfloat16 [16384, 6144], P('ctx', 'head'), may hold values from -6 to 6
- delta_key: bfloat16 [16384, 6144], P('ctx', 'head'), may hold values from -6 to 6
- delta_value: bfloat16 [16384, 6144], P('ctx', 'head'), may hold values from -120 to 120
- delta_gate: float32 [16384, 48], P('ctx', 'head'), may hold values from 0.5 to 1
- delta_beta: float32 [16384, 48], P('ctx', 'head'), may hold values from 0 to 0.6, as said below
- attn_gain: float32 [6144], P('head'), may hold values from 0.1 to 1.9
- delta_gain: float32 [6144], P('head'), may hold values from 0.1 to 1.9
Outputs:
- mixed: bfloat16 [16384, 6144], P('ctx', 'head')
The draws below stay inside these ranges and needn't reach their ends.
Inputs may be any that keep to these rules, and one draw needn't show every extreme that they name: `delta_beta`: Positive.
All inputs are finite; a program needn't handle non-finite values.
Results may differ from the reference program's by a relative error of at most 0.004.
Values may be sent and summed in bfloat16 or wider, within the bound.
No kernel may reach another device: no remote copies, remote signals or barrier semaphores. Data moves between devices by JAX's collectives and lax.ppermute only.
A program may use at most 192 MiB of HBM per device.

```python
import math
import jax
import jax.numpy as jnp
from jax import lax

HEAD_COUNT = 48
DH = 128
WIDTH = 6144
WINDOW = 1024
GROUP = 64
TOK_DEV = 512
TOKEN_COUNT = 16384


def drawn_pair(key):
    sequence_lanes = jax.random.split(jax.random.fold_in(key, 101), 2)
    queries = jnp.clip(jax.random.normal(sequence_lanes[0], (TOKEN_COUNT, HEAD_COUNT, DH), jnp.float32), -5.0, 5.0)
    keyvecs = jnp.clip(jax.random.normal(sequence_lanes[1], (TOKEN_COUNT, HEAD_COUNT, DH), jnp.float32), -5.0, 5.0)
    return (queries.reshape(TOKEN_COUNT, HEAD_COUNT * DH), keyvecs.reshape(TOKEN_COUNT, HEAD_COUNT * DH))


def scaled_values(key, salt):
    sequence_lanes = jax.random.split(jax.random.fold_in(key, salt), 1)
    values = jnp.clip(jax.random.normal(sequence_lanes[0], (TOKEN_COUNT, HEAD_COUNT, DH), jnp.float32), -4.0, 4.0)
    head_ramp = jnp.exp(math.log(3.0) * jnp.arange(HEAD_COUNT, dtype=jnp.float32) / max(HEAD_COUNT - 1, 1))
    values = values * head_ramp[None, :, None]
    return values.reshape(TOKEN_COUNT, HEAD_COUNT * DH)


def fast_heads(key):
    fraction = 0.5
    return jax.random.bernoulli(jax.random.fold_in(key, 202), fraction, (HEAD_COUNT,))


def draw_attn_query(key, part):
    return drawn_pair(key)[0].astype(jnp.bfloat16)


def draw_attn_key(key, part):
    return drawn_pair(key)[1].astype(jnp.bfloat16)


def draw_attn_value(key, part):
    return scaled_values(key, 303).astype(jnp.bfloat16)


def draw_delta_value(key, part):
    return scaled_values(key, 404).astype(jnp.bfloat16)


def draw_delta_key(key, part):
    rapid_heads = fast_heads(key)
    sequence_lanes = jax.random.split(jax.random.fold_in(key, 707), 3)
    sub_dims = max(DH * 3 // 16, 2)
    shard_count = TOKEN_COUNT // TOK_DEV
    background = jax.random.normal(sequence_lanes[0], (shard_count, TOK_DEV, HEAD_COUNT, DH), jnp.float32)
    directions = jax.random.normal(sequence_lanes[1], (shard_count, HEAD_COUNT, sub_dims, DH), jnp.float32) / math.sqrt(DH)
    loadings = jax.random.normal(sequence_lanes[2], (shard_count, TOK_DEV, HEAD_COUNT, sub_dims), jnp.float32)
    focused = 4.0 * jnp.einsum('bths,bhsd->bthd', loadings, directions)
    keyvecs = background + jnp.where(rapid_heads[None, None, :, None], 0.0, focused)
    keyvecs = jnp.clip(keyvecs, -6.0, 6.0)
    return keyvecs.reshape(TOKEN_COUNT, HEAD_COUNT * DH).astype(jnp.bfloat16)


def draw_delta_gate(key, part):
    rapid_heads = fast_heads(key)
    sequence_lanes = jax.random.split(jax.random.fold_in(key, 505), 3)
    roughness = jnp.exp(jax.random.uniform(sequence_lanes[0], (TOKEN_COUNT, HEAD_COUNT), jnp.float32, math.log(0.5), math.log(2.0)))
    log_decay_rates = jnp.where(rapid_heads[None, :], 1.0 / 40.0, 0.5 / TOKEN_COUNT) * roughness
    token_groups = jax.random.bernoulli(sequence_lanes[1], 2.0 / TOKEN_COUNT, (TOKEN_COUNT, HEAD_COUNT)) & jnp.logical_not(rapid_heads)[None, :]
    removed_entries = jax.random.uniform(sequence_lanes[2], (TOKEN_COUNT, HEAD_COUNT), jnp.float32, 0.5, 0.8)
    return jnp.where(token_groups, removed_entries, jnp.exp(-log_decay_rates)).astype(jnp.float32)


def draw_delta_beta(key, part):
    rapid_heads = fast_heads(key)
    roughness = jnp.exp(jax.random.uniform(jax.random.fold_in(key, 606), (TOKEN_COUNT, HEAD_COUNT), jnp.float32, math.log(0.5), math.log(2.0)))
    baseline = jnp.where(rapid_heads[None, :], 0.25, float(DH) / TOKEN_COUNT)
    return jnp.minimum(baseline * roughness, 0.6).astype(jnp.float32)


def steps_of(own_key, extent, cuts, low, high):
    gain = 1.0
    for dim, shards_of in cuts:
        steps = jax.random.uniform(jax.random.fold_in(jax.random.fold_in(own_key, 6), dim), (shards_of,), jnp.float32, low / len(cuts), high / len(cuts))
        gain = gain * jnp.repeat(jnp.exp(steps), extent[dim] // shards_of).reshape((-1,) + (1,) * (len(extent) - 1 - dim))
    return gain


def normal_values(rng, shape, scale, limit, cuts=(), held_as=jnp.bfloat16):
    gain = steps_of(rng, shape, cuts, -0.22, 0.18) if cuts else 1.0
    values = jax.random.normal(rng, shape, jnp.float32) * scale * gain
    return jnp.minimum(jnp.maximum(values, -limit), limit).astype(held_as)


def setup_inputs(seed: int = 0) -> dict:
    keys = jax.random.split(jax.random.key(seed), 11)
    return {
        "attn_query": draw_attn_query(jax.random.fold_in(keys[10], 71), 0),
        "attn_key": draw_attn_key(jax.random.fold_in(keys[10], 71), 0),
        "attn_value": draw_attn_value(jax.random.fold_in(keys[10], 71), 0),
        "delta_query": normal_values(keys[3], (TOKEN_COUNT, WIDTH), 1.0, 6.0, ((0, 32), (1, 4))),
        "delta_key": draw_delta_key(jax.random.fold_in(keys[10], 71), 0),
        "delta_value": draw_delta_value(jax.random.fold_in(keys[10], 71), 0),
        "delta_gate": draw_delta_gate(jax.random.fold_in(keys[10], 71), 0),
        "delta_beta": draw_delta_beta(jax.random.fold_in(keys[10], 71), 0),
        "attn_gain": jnp.clip(1.0 + 0.18 * jax.random.normal(keys[8], (WIDTH,), jnp.float32), 0.1, 1.9),
        "delta_gain": jnp.clip(1.0 + 0.18 * jax.random.normal(keys[9], (WIDTH,), jnp.float32), 0.1, 1.9),
    }


epsilon = 1e-06
highest = lax.Precision.HIGHEST

def unit_rows(values):
    return values * lax.rsqrt(lax.optimization_barrier(jnp.mean(values * values, axis=-1, keepdims=True)) + epsilon) / math.sqrt(values.shape[-1])

def group_terms(inputs):
    queries, keyvecs, values, alphas, betas = inputs
    length = alphas.shape[0]
    log_sums = jnp.cumsum(jnp.log(alphas), axis=0)
    causal = jnp.arange(length, dtype=jnp.int32)[:, None] >= jnp.arange(length, dtype=jnp.int32)[None, :]
    spread = log_sums.T[:, :, None] - log_sums.T[:, None, :]
    ratios = jnp.exp(jnp.where(causal[None], spread, -1e+30))
    identity = jnp.eye(length, dtype=jnp.float32)
    key_gram = jnp.einsum('rhd,shd->hrs', keyvecs, keyvecs, precision=highest)
    negated = -(betas.T[:, :, None] * ratios * (1.0 - identity) * key_gram)
    inverse = identity + negated
    powered = negated
    for doubling in range(max((length - 1).bit_length() - 1, 0)):
        powered = jnp.einsum('hij,hjk->hik', powered, powered, precision=highest)
        inverse = inverse + jnp.einsum('hij,hjk->hik', inverse, powered, precision=highest)
    growth = jnp.exp(log_sums)
    scaled_vals = jnp.transpose(betas[:, :, None] * values, (1, 0, 2))
    scaled_keys = jnp.transpose((betas * growth)[:, :, None] * keyvecs, (1, 0, 2))
    pseudo_vals = jnp.einsum('hij,hjd->hid', inverse, scaled_vals, precision=highest)
    pseudo_keys = jnp.einsum('hij,hjd->hid', inverse, scaled_keys, precision=highest)
    decay_tail = jnp.exp(log_sums[-1][:, None] - log_sums.T)
    return (log_sums, ratios, growth, decay_tail, pseudo_vals, pseudo_keys)

def group_step(current, inputs):
    queries, keyvecs, values, alphas, betas = inputs
    log_sums, ratios, growth, decay_tail, pseudo_vals, pseudo_keys = group_terms(inputs)
    errors = pseudo_vals - jnp.einsum('hcd,hde->hce', pseudo_keys, current, precision=highest)
    mixing = jnp.einsum('rhd,shd->hrs', queries, keyvecs, precision=highest) * ratios
    outputs = growth.T[:, :, None] * jnp.einsum('chd,hde->hce', queries, current, precision=highest)
    outputs = outputs + jnp.einsum('hrs,hse->hre', mixing, errors, precision=highest)
    new_state = jnp.exp(log_sums[-1])[:, None, None] * current
    new_state = new_state + jnp.einsum('chd,hc,hce->hde', keyvecs, decay_tail, errors, precision=highest)
    return (new_state, jnp.transpose(outputs, (1, 0, 2)))

def delta_inputs(queries, keyvecs, values, alphas, betas):
    length = alphas.shape[0]
    count = alphas.shape[1]
    blocks = length // GROUP

    def to_blocks(array):
        return array.astype(jnp.float32).reshape(blocks, GROUP, count, DH)
    return (unit_rows(to_blocks(queries)), unit_rows(to_blocks(keyvecs)), to_blocks(values), alphas.reshape(blocks, GROUP, count), betas.reshape(blocks, GROUP, count))

def attend(queries, keyvecs, values, query_start, key_start):
    scores = jnp.einsum('qhd,khd->hqk', queries.astype(jnp.float32), keyvecs.astype(jnp.float32)) / math.sqrt(queries.shape[-1])
    query_pos = query_start + jnp.arange(queries.shape[0], dtype=jnp.int32)[:, None]
    key_pos = key_start + jnp.arange(keyvecs.shape[0], dtype=jnp.int32)[None, :]
    distance = query_pos - key_pos
    allowed = (distance >= 0) & (distance < WINDOW) & (key_pos >= 0)
    scores = jnp.where(allowed[None], scores, -1e+30)
    maxima = lax.optimization_barrier(jnp.max(scores, axis=-1, keepdims=True))
    raised = jnp.exp(scores - maxima)
    weights = (raised / lax.optimization_barrier(jnp.sum(raised, axis=-1, keepdims=True))).astype(jnp.bfloat16)
    return jnp.einsum('hqk,khd->qhd', weights.astype(jnp.float32), values.astype(jnp.float32))

def window_attention(queries, keyvecs, values):
    length = queries.shape[0]
    block_rows = math.gcd(length, 512)
    padded_keys = jnp.concatenate([jnp.zeros((WINDOW, WIDTH), jnp.bfloat16), keyvecs], axis=0)
    padded_vals = jnp.concatenate([jnp.zeros((WINDOW, WIDTH), jnp.bfloat16), values], axis=0)

    def one_block(start):
        query_blk = lax.dynamic_slice_in_dim(queries, start, block_rows, 0).reshape(block_rows, HEAD_COUNT, DH)
        key_blk = lax.dynamic_slice_in_dim(padded_keys, start, block_rows + WINDOW, 0).reshape(block_rows + WINDOW, HEAD_COUNT, DH)
        value_blk = lax.dynamic_slice_in_dim(padded_vals, start, block_rows + WINDOW, 0).reshape(block_rows + WINDOW, HEAD_COUNT, DH)
        return attend(query_blk, key_blk, value_blk, start, start - WINDOW)
    starts = jnp.arange(length // block_rows, dtype=jnp.int32) * block_rows
    outputs = lax.map(one_block, starts)
    return outputs.reshape(length, WIDTH)

def reference(attn_query, attn_key, attn_value, delta_query, delta_key, delta_value, delta_gate, delta_beta, attn_gain, delta_gain):
    attn_out = window_attention(attn_query, attn_key, attn_value)
    prepared = delta_inputs(delta_query, delta_key, delta_value, delta_gate, delta_beta)
    current = jnp.zeros((HEAD_COUNT, DH, DH), jnp.float32)
    final_state, delta_blocks = lax.scan(group_step, current, prepared)
    delta_out = delta_blocks.reshape(TOKEN_COUNT, WIDTH)
    scale_attn = lax.rsqrt(lax.optimization_barrier(jnp.mean(attn_out * attn_out, axis=-1, keepdims=True)) + epsilon)
    scale_delta = lax.rsqrt(lax.optimization_barrier(jnp.mean(delta_out * delta_out, axis=-1, keepdims=True)) + epsilon)
    joined = 0.5 * (attn_gain * attn_out * scale_attn + delta_gain * delta_out * scale_delta)
    return joined.astype(jnp.bfloat16)
```

```python
import functools
import math

import jax
import jax.numpy as jnp
from jax import lax
from jax.experimental import pallas as pl
from jax.experimental.pallas import tpu as pltpu
from jax.sharding import PartitionSpec as P

DH = 128
WIDTH = 6144
WINDOW = 1024
EPS = 1e-06
C = 128
HB = 2
PAY = 208
NEG = -1e30
f32 = jnp.float32
bf16 = jnp.bfloat16

NN = (((1,), (0,)), ((), ()))
NT = (((1,), (1,)), ((), ()))
TN = (((0,), (0,)), ((), ()))


def mm(a, b, dims=NN):
    return lax.dot_general(a, b, dims, preferred_element_type=f32)


def split(x):
    hi = x.astype(bf16)
    lo = (x - hi.astype(f32)).astype(bf16)
    return hi, lo


def cat(parts, axis):
    return jnp.concatenate(parts, axis=axis)


def dot3(a, b):
    (ah, al), (bh, bl) = a, b
    lhs = cat([ah, al], 1)
    rhs = cat([cat([bh, bl], 1), cat([bh, jnp.zeros_like(bl)], 1)], 0)
    r = mm(lhs, rhs)
    return r[:, :C] + r[:, C:]


def wide3(a, b):
    (ah, al), (bh, bl) = a, b
    return mm(cat([ah, al], 1), cat([bh, bh], 0)) + mm(ah, bl)


def delta_kernel(q_ref, k_ref, v_ref, g_ref, b_ref, o_ref, y_ref, pay_ref):
    rows = q_ref.shape[0]
    nc = rows // C
    units = HB * nc
    ri = lax.broadcasted_iota(jnp.int32, (C, C), 0)
    ci = lax.broadcasted_iota(jnp.int32, (C, C), 1)
    eye = ri == ci
    lower = ri >= ci
    xor = jnp.where(ri > ci, ri ^ ci, 0)
    triu = jnp.where(ri <= ci, 1.0, 0.0).astype(f32)
    identity = jnp.where(eye, 1.0, 0.0).astype(f32)

    def rows_of(ref):
        return cat([ref[hh][:, c * C : (c + 1) * C] for hh in range(HB) for c in range(nc)], 0)

    def tile(ref, hh, c):
        return ref[c * C : (c + 1) * C, hh * DH : (hh + 1) * DH]

    pairs = [(hh, c) for hh in range(HB) for c in range(nc)]
    logs = lax.dot_general(
        jnp.log(rows_of(g_ref)), triu, NN, precision=lax.Precision.HIGHEST, preferred_element_type=f32
    )
    beta = rows_of(b_ref)
    grams = []
    for hh, c in pairs:
        k = tile(k_ref, hh, c)
        grams.append(mm(cat([k, tile(q_ref, hh, c)], 0), k, NT))
    diag = cat([jnp.sum(jnp.where(eye, g[:C], 0.0), axis=0, keepdims=True) for g in grams], 0)
    key_scale = lax.rsqrt(diag * (1.0 / DH) + EPS) * (1.0 / math.sqrt(DH))
    growth = jnp.exp(logs)
    last = logs[:, C - 1 : C]
    decay = jnp.exp(last)
    tail = jnp.exp(last - logs) * key_scale
    bs = beta * key_scale
    logs_c, growth_c, tail_c, bs_c, beta_c, bgs_c = (
        jnp.transpose(x) for x in (logs, growth, tail, bs, beta, bs * growth)
    )

    negs, mixes, invs = [], [], []
    for u, (hh, c) in enumerate(pairs):
        col = slice(u, u + 1)
        ratio = jnp.exp(jnp.where(lower, logs_c[:, col] - logs[col, :], NEG)) * key_scale[col, :]
        neg = jnp.where(xor > 0, grams[u][:C] * ratio * (-bs_c[:, col]), 0.0)
        mixes.append(split(grams[u][C:] * ratio))
        negs.append(split(neg))
        invs.append(identity + jnp.where(xor == 1, neg, 0.0))
    for level in range(1, C.bit_length() - 1):
        mask = (xor >> level) == 1
        parts = [split(t) for t in invs]
        left = [dot3(parts[u], negs[u]) for u in range(units)]
        both = [dot3(split(left[u]), parts[u]) for u in range(units)]
        invs = [invs[u] + jnp.where(mask, both[u], 0.0) for u in range(units)]
    invs = [split(t) for t in invs]

    zero = jnp.zeros((C, DH), f32)
    states = [None] * HB
    for c in range(nc):
        for hh in range(HB):
            u = hh * nc + c
            col = slice(u, u + 1)
            k, q, v = tile(k_ref, hh, c), tile(q_ref, hh, c), tile(v_ref, hh, c)
            vb = cat([v.astype(f32) * beta_c[:, col], zero], 1)
            if c == 0:
                ks = cat([zero, k.astype(f32)], 1)
                qs = cat([zero, q.astype(f32)], 1)
            else:
                sh, sl = split(states[hh])
                kq = cat([k, q], 0)
                both = mm(cat([kq, kq], 1), cat([sh, sl], 0))
                ks, qs = both[:C], both[C:]
            err = wide3(invs[u], split(vb - bgs_c[:, col] * ks))
            out = growth_c[:, col] * qs + wide3(mixes[u], split(err))
            qf = q.astype(f32)
            q_scale = lax.rsqrt(jnp.mean(qf * qf, axis=1, keepdims=True) + EPS) * (1.0 / math.sqrt(DH))
            out = out * q_scale
            o_ref[c * C : (c + 1) * C, hh * DH : (hh + 1) * DH] = out[:, :DH]
            y_ref[c * C : (c + 1) * C, hh * DH : (hh + 1) * DH] = out[:, DH:]
            eh, el = split(err * tail_c[:, col])
            new = mm(cat([k, k], 0), cat([eh, el], 0), TN)
            if c == 0:
                start = cat([zero, identity], 1)
                states[hh] = new + decay[u : u + 1, :] * start
            else:
                states[hh] = new + decay[u : u + 1, :] * states[hh]

    row16 = lax.broadcasted_iota(jnp.int32, (16, DH), 0)
    for hh in range(HB):
        total = decay[hh * nc : hh * nc + 1, :]
        for c in range(1, nc):
            total = total * decay[hh * nc + c : hh * nc + c + 1, :]
        linear = (states[hh][:, DH:] - total * identity).astype(bf16)
        offset = jnp.transpose(states[hh][:, :DH]).astype(bf16)
        wide = jnp.broadcast_to(total, (16, DH))
        th = wide.astype(bf16).astype(f32)
        decays = jnp.where(row16 == 0, th, jnp.where(row16 == 1, wide - th, 0.0)).astype(bf16)
        for half in range(2):
            pay_ref[2 * hh + half, 0:128, :] = linear
            pay_ref[2 * hh + half, 128:192, :] = offset[half * 64 : (half + 1) * 64]
            pay_ref[2 * hh + half, 192:208, :] = decays


def chain_kernel(in_ref, out_ref):
    n = in_ref.shape[0]
    state = jnp.zeros((64, DH), f32)
    for j in range(n):
        out_ref[j] = state
        if j == n - 1:
            break
        sh, sl = split(state)
        r = mm(cat([sh, sl], 0), in_ref[j, 0:128, :], NT)
        dec = in_ref[j, 192:208, :].astype(f32)
        total = dec[0:1] + dec[1:2]
        state = r[:64] + r[64:] + total * state + in_ref[j, 128:192, :].astype(f32)


def attn_kernel(idx_ref, q_ref, k0_ref, v0_ref, k1a_ref, v1a_ref, k1b_ref, v1b_ref, k2_ref, v2_ref, o_ref, s_ref, k1_ref, v1_ref):
    QB = 128
    rows = q_ref.shape[0]
    nb = rows // QB
    ctx = idx_ref[0]
    odd = lax.rem(ctx, 2) == 1
    scale = math.log2(math.e) / math.sqrt(DH)

    @pl.when(odd)
    def _():
        k1_ref[...] = k1a_ref[...]
        v1_ref[...] = v1a_ref[...]

    @pl.when(jnp.logical_not(odd))
    def _():
        k1_ref[...] = k1b_ref[...]
        v1_ref[...] = v1b_ref[...]

    bias1 = jnp.where(ctx >= 1, 0.0, 1e30).astype(f32)
    bias2 = jnp.where(ctx >= 2, 0.0, 1e30).astype(f32)
    ri = lax.broadcasted_iota(jnp.int32, (QB, QB), 0)
    ci = lax.broadcasted_iota(jnp.int32, (QB, QB), 1)
    far = ci > ri

    @pl.when(pl.program_id(0) == 0)
    def _():
        s_ref[...] = jnp.zeros_like(s_ref)

    for b in range(nb):
        q = q_ref[b * QB : (b + 1) * QB, :]
        s2 = mm(q, k2_ref[b * QB :, :], NT)
        s1 = mm(q, k1_ref[...], NT)
        s0 = mm(q, k0_ref[: (b + 1) * QB, :], NT)
        st = jnp.where(far, s2[:, :QB] - bias2, s0[:, b * QB :])
        top = jnp.max(st, axis=1, keepdims=True)
        top = jnp.maximum(top, jnp.max(s1, axis=1, keepdims=True) - bias1)
        if b < nb - 1:
            s2 = s2[:, QB:]
            top = jnp.maximum(top, jnp.max(s2, axis=1, keepdims=True) - bias2)
        if b > 0:
            s0 = s0[:, : b * QB]
            top = jnp.maximum(top, jnp.max(s0, axis=1, keepdims=True))
        pt = jnp.exp2((st - top) * scale)
        p1 = jnp.exp2((s1 - (top + bias1)) * scale)
        total = jnp.sum(pt, axis=1, keepdims=True) + jnp.sum(p1, axis=1, keepdims=True)
        if b < nb - 1:
            p2 = jnp.exp2((s2 - (top + bias2)) * scale)
            total = total + jnp.sum(p2, axis=1, keepdims=True)
        if b > 0:
            p0 = jnp.exp2((s0 - top) * scale)
            total = total + jnp.sum(p0, axis=1, keepdims=True)
        inv = 1.0 / total
        pt = pt * inv
        w2 = jnp.where(far, pt, 0.0).astype(bf16)
        w0 = jnp.where(far, 0.0, pt).astype(bf16)
        if b < nb - 1:
            w2 = cat([w2, (p2 * inv).astype(bf16)], 1)
        if b > 0:
            w0 = cat([(p0 * inv).astype(bf16), w0], 1)
        w1 = (p1 * inv).astype(bf16)
        out = mm(w1, v1_ref[...]) + mm(w2, v2_ref[b * QB :, :]) + mm(w0, v0_ref[: (b + 1) * QB, :])
        o_ref[b * QB : (b + 1) * QB, :] = out
        s_ref[b * QB : (b + 1) * QB, :] += out * out


def apply_kernel(o_ref, y_ref, t_ref, d_ref, s_ref):
    yh, yl = split(y_ref[...])
    s = cat([t_ref[0], t_ref[1]], 0)
    sh, sl = split(s)
    out = o_ref[...] + mm(cat([yh, yl], 1), cat([sh, sh], 1), NT) + mm(yh, sl, NT)
    d_ref[...] = out

    @pl.when(pl.program_id(0) == 0)
    def _():
        s_ref[...] = jnp.zeros_like(s_ref)

    s_ref[...] += out * out


def join_kernel(sq_ref, a_ref, d_ref, ag_ref, dg_ref, o_ref):
    sq = sq_ref[...]
    scale = lax.rsqrt(sq * (1.0 / WIDTH) + EPS)
    o_ref[...] = (
        0.5 * (ag_ref[...] * a_ref[...] * scale[:, 0:1] + dg_ref[...] * d_ref[...] * scale[:, 1:2])
    ).astype(bf16)


def params(mb):
    return pltpu.CompilerParams(vmem_limit_bytes=mb * 2**20)


def on_device(aq, ak, av, dq, dk, dv, gate, beta, ag, dg):
    rows, width = aq.shape
    heads = gate.shape[1]
    nctx = lax.axis_size("ctx")
    index = lax.axis_index("ctx").astype(jnp.int32).reshape(1)

    hop = [(i, i + 2) for i in range(nctx - 2)]
    ahead = [(i, i + 1) for i in range(0, nctx, 2)]
    back = [(i, i - 1) for i in range(1, nctx, 2)]

    def send(x, pairs):
        return lax.ppermute(x, "ctx", pairs)

    k2, v2 = send(ak, hop), send(av, hop)
    k1a, v1a = send(ak, ahead), send(av, ahead)
    k1b, v1b = send(k2, back), send(v2, back)

    gt = gate.T.reshape(heads, 1, rows)
    bt = beta.T.reshape(heads, 1, rows)
    wide = pl.BlockSpec((rows, HB * DH), lambda h: (0, h))
    small = pl.BlockSpec((HB, 1, rows), lambda h: (h, 0, 0))
    local, effect, pay = pl.pallas_call(
        delta_kernel,
        grid=(heads // HB,),
        in_specs=[wide, wide, wide, small, small],
        out_specs=[wide, wide, pl.BlockSpec((2 * HB, PAY, DH), lambda h: (h, 0, 0))],
        out_shape=[
            jax.ShapeDtypeStruct((rows, width), f32),
            jax.ShapeDtypeStruct((rows, width), f32),
            jax.ShapeDtypeStruct((nctx, PAY, DH), bf16),
        ],
        compiler_params=params(48),
        cost_estimate=pl.CostEstimate(flops=30 * 10**9, bytes_accessed=12 * 2**20, transcendentals=10**6),
        name="delta_local",
    )(dq, dk, dv, gt, bt)

    got = lax.all_to_all(pay, "ctx", 0, 0, tiled=True)
    chain = pl.pallas_call(
        chain_kernel,
        out_shape=jax.ShapeDtypeStruct((nctx, 64, DH), f32),
        compiler_params=params(32),
        cost_estimate=pl.CostEstimate(flops=10**10, bytes_accessed=3 * 2**20, transcendentals=0),
        name="delta_chain",
    )(got)
    states = lax.all_to_all(chain, "ctx", 0, 0, tiled=True)

    one = pl.BlockSpec((rows, DH), lambda h: (0, h))
    fixed = pl.BlockSpec((rows, DH), lambda h: (0, 0))
    attn, attn_sq = pl.pallas_call(
        attn_kernel,
        grid=(heads,),
        in_specs=[pl.BlockSpec(memory_space=pltpu.SMEM)] + [one] * 9,
        out_specs=[one, fixed],
        out_shape=[
            jax.ShapeDtypeStruct((rows, width), f32),
            jax.ShapeDtypeStruct((rows, DH), f32),
        ],
        scratch_shapes=[pltpu.VMEM((rows, DH), bf16), pltpu.VMEM((rows, DH), bf16)],
        compiler_params=params(48),
        cost_estimate=pl.CostEstimate(flops=10**10, bytes_accessed=20 * 2**20, transcendentals=7 * 10**6),
        name="window_attention",
    )(index, aq, ak, av, k1a, v1a, k1b, v1b, k2, v2)

    delta, delta_sq = pl.pallas_call(
        apply_kernel,
        grid=(heads,),
        in_specs=[one, one, pl.BlockSpec((2, 64, DH), lambda h: (h, 0, 0))],
        out_specs=[one, fixed],
        out_shape=[
            jax.ShapeDtypeStruct((rows, width), f32),
            jax.ShapeDtypeStruct((rows, DH), f32),
        ],
        compiler_params=params(32),
        name="delta_apply",
    )(local, effect, states)

    squares = jnp.stack([jnp.sum(attn_sq, axis=1), jnp.sum(delta_sq, axis=1)], axis=1)
    squares = lax.psum(squares, "head")

    block = 256
    cols = pl.BlockSpec((block, width), lambda i: (i, 0))
    gains = pl.BlockSpec((1, width), lambda i: (0, 0))
    return pl.pallas_call(
        join_kernel,
        grid=(rows // block,),
        in_specs=[pl.BlockSpec((block, 2), lambda i: (i, 0)), cols, cols, gains, gains],
        out_specs=cols,
        out_shape=jax.ShapeDtypeStruct((rows, width), bf16),
        compiler_params=params(32),
        name="join",
    )(squares, attn, delta, ag.reshape(1, width), dg.reshape(1, width))


def solution(mesh):
    shard = P("ctx", "head")
    return jax.shard_map(
        on_device,
        mesh=mesh,
        in_specs=(shard,) * 8 + (P("head"), P("head")),
        out_specs=shard,
        check_vma=False,
    )
```

```python
import functools
import math

import jax
import jax.numpy as jnp
from jax import lax
from jax.experimental import pallas as pl
from jax.experimental.pallas import tpu as pltpu
from jax.sharding import PartitionSpec as P

DH = 128
WIDTH = 6144
WINDOW = 1024
EPS = 1e-06
C = 128
PARTS = (6, 4, 2)
AH = 2
QB = 256
COSTS = (2, 8, 5, 10, 5)
PAY = 208
NEG = -1e30
f32 = jnp.float32
bf16 = jnp.bfloat16

NN = (((1,), (0,)), ((), ()))
NT = (((1,), (1,)), ((), ()))
TN = (((0,), (0,)), ((), ()))


def mm(a, b, dims=NN):
    return lax.dot_general(a, b, dims, preferred_element_type=f32)


def split(x):
    hi = x.astype(bf16)
    lo = (x - hi.astype(f32)).astype(bf16)
    return hi, lo


def cat(parts, axis):
    return jnp.concatenate(parts, axis=axis)


def dot3(a, b):
    (ah, al), (bh, bl) = a, b
    lhs = cat([ah, al], 1)
    rhs = cat([cat([bh, bl], 1), cat([bh, jnp.zeros_like(bl)], 1)], 0)
    r = mm(lhs, rhs)
    return r[:, :C] + r[:, C:]


def wide3(a, b):
    (ah, al), (bh, bl) = a, b
    return mm(cat([ah, al], 1), cat([bh, bh], 0)) + mm(ah, bl)


def block_rows(ref, c):
    return cat([ref[hh][:, c * C : (c + 1) * C] for hh in range(ref.shape[0])], 0)


def tile(ref, hh, c):
    return ref[c * C : (c + 1) * C, hh * DH : (hh + 1) * DH]


def iotas():
    ri = lax.broadcasted_iota(jnp.int32, (C, C), 0)
    ci = lax.broadcasted_iota(jnp.int32, (C, C), 1)
    return ri, ci


def pair_list(hb, nc):
    return [(hh, c) for hh in range(hb) for c in range(nc)]


def log_sums(g_ref, pairs, ri, ci):
    triu = jnp.where(ri <= ci, 1.0, 0.0).astype(f32)
    rows = cat([g_ref[hh][:, c * C : (c + 1) * C] for hh, c in pairs], 0)
    return lax.dot_general(
        jnp.log(rows), triu, NN, precision=lax.Precision.HIGHEST, preferred_element_type=f32
    )


def map_kernel(k_ref, v_ref, g_ref, b_ref, uw_ref, s_ref, l_ref, pay_ref):
    rows = k_ref.shape[0]
    hb = g_ref.shape[0]
    nc = rows // C
    units = range(hb * nc)
    pairs = pair_list(hb, nc)
    ri, ci = iotas()
    eye = ri == ci
    xor = jnp.where(ri > ci, ri ^ ci, 0)
    identity = jnp.where(eye, 1.0, 0.0).astype(f32)

    logs = log_sums(g_ref, pairs, ri, ci)
    beta = cat([b_ref[hh][:, c * C : (c + 1) * C] for hh, c in pairs], 0)
    keys = [tile(k_ref, hh, c) for hh, c in pairs]
    grams = [mm(k, k, NT) for k in keys]
    diag = cat([jnp.sum(jnp.where(eye, g, 0.0), axis=0, keepdims=True) for g in grams], 0)
    key_scale = lax.rsqrt(diag * (1.0 / DH) + EPS) * (1.0 / math.sqrt(DH))
    growth = jnp.exp(logs)
    last = logs[:, C - 1 : C]
    decay = jnp.exp(last)
    tail = jnp.exp(last - logs) * key_scale
    bs = beta * key_scale
    logs_c, tail_c, bs_c, beta_c, bgs_c = (
        jnp.transpose(x) for x in (logs, tail, bs, beta, bs * growth)
    )
    for u, (hh, c) in enumerate(pairs):
        l_ref[hh, c] = jnp.broadcast_to(logs[u : u + 1], (8, C))
        l_ref[hh, nc + c] = jnp.broadcast_to(key_scale[u : u + 1], (8, C))

    negs, invs = [], []
    for u in units:
        col = slice(u, u + 1)
        ratio = jnp.exp(jnp.where(ri > ci, logs_c[:, col] - logs[col, :], NEG)) * key_scale[col, :]
        neg = grams[u] * ratio * (-bs_c[:, col])
        negs.append(split(neg))
        invs.append(identity + jnp.where(xor == 1, neg, 0.0))
    for level in range(1, C.bit_length() - 1):
        mask = (xor >> level) == 1
        parts = [split(t) for t in invs]
        left = [dot3(parts[u], negs[u]) for u in units]
        both = [dot3(split(left[u]), parts[u]) for u in units]
        invs = [invs[u] + jnp.where(mask, both[u], 0.0) for u in units]
    invs = [split(t) for t in invs]

    right = []
    for u, (hh, c) in enumerate(pairs):
        col = slice(u, u + 1)
        v = tile(v_ref, hh, c).astype(f32) * beta_c[:, col]
        k = keys[u].astype(f32) * bgs_c[:, col]
        right.append(split(cat([v, k], 1)))
    fixed = [wide3(invs[u], right[u]) for u in units]
    for u, (hh, c) in enumerate(pairs):
        uw_ref[hh, c] = fixed[u].astype(bf16)
    turned = [jnp.transpose(k) for k in keys]
    ends = [split(fixed[u] * tail_c[:, u : u + 1]) for u in units]
    maps = [mm(cat([turned[u], turned[u]], 1), cat(ends[u], 0)) for u in units]
    zero = jnp.zeros((C, DH), f32)
    start = cat([zero, identity], 1)

    states = []
    for hh in range(hb):
        u = hh * nc
        m = maps[u]
        states.append(cat([m[:, :DH], decay[u : u + 1, :] * identity - m[:, DH:]], 1))
    for c in range(1, nc):
        parts = [split(s) for s in states]
        for hh in range(hb):
            s_ref[hh, c - 1] = states[hh].astype(bf16)
        moved = [wide3(split(maps[hh * nc + c][:, DH:]), parts[hh]) for hh in range(hb)]
        for hh in range(hb):
            u = hh * nc + c
            offset = cat([maps[u][:, :DH], zero], 1)
            states[hh] = decay[u : u + 1, :] * states[hh] + (offset - moved[hh])

    row16 = lax.broadcasted_iota(jnp.int32, (16, DH), 0)
    for hh in range(hb):
        total = decay[hh * nc : hh * nc + 1, :]
        for c in range(1, nc):
            total = total * decay[hh * nc + c : hh * nc + c + 1, :]
        linear = (states[hh][:, DH:] - total * identity).astype(bf16)
        offset = jnp.transpose(states[hh][:, :DH]).astype(bf16)
        wide = jnp.broadcast_to(total, (16, DH))
        th = wide.astype(bf16).astype(f32)
        decays = jnp.where(row16 == 0, th, jnp.where(row16 == 1, wide - th, 0.0)).astype(bf16)
        for half in range(2):
            pay_ref[2 * hh + half, 0:128, :] = linear
            pay_ref[2 * hh + half, 128:192, :] = offset[half * 64 : (half + 1) * 64]
            pay_ref[2 * hh + half, 192:208, :] = decays


def out_kernel(q_ref, k_ref, uw_ref, l_ref, o_ref, y_ref):
    rows = q_ref.shape[0]
    hb = uw_ref.shape[0]
    nc = rows // C
    pairs = pair_list(hb, nc)
    ri, ci = iotas()
    lower = ri >= ci
    raw = [mm(tile(q_ref, hh, c), tile(k_ref, hh, c), NT) for hh, c in pairs]
    inner, growth = [], []
    for u, (hh, c) in enumerate(pairs):
        log_row, key_scale = l_ref[hh, c][0:1], l_ref[hh, nc + c][0:1]
        logs_c = jnp.transpose(l_ref[hh, c])[:, 0:1]
        mh, ml = split(raw[u] * (jnp.exp(jnp.where(lower, logs_c - log_row, NEG)) * key_scale))
        uw = uw_ref[hh, c]
        inner.append(mm(cat([mh, ml], 1), cat([uw, uw], 0)))
        growth.append(jnp.exp(logs_c))
    for u, (hh, c) in enumerate(pairs):
        qf = tile(q_ref, hh, c).astype(f32)
        scale = lax.rsqrt(jnp.mean(qf * qf, axis=1, keepdims=True) + EPS) * (1.0 / math.sqrt(DH))
        at = (slice(c * C, (c + 1) * C), slice(hh * DH, (hh + 1) * DH))
        o_ref[at] = inner[u][:, :DH] * scale
        y_ref[at] = ((growth[u] * qf - inner[u][:, DH:]) * scale).astype(bf16)


def chain_kernel(in_ref, out_ref):
    n = in_ref.shape[0]
    state = jnp.zeros((64, DH), f32)
    for j in range(n):
        out_ref[j] = state.astype(out_ref.dtype)
        if j == n - 1:
            break
        sh, sl = split(state)
        r = mm(cat([sh, sl], 0), in_ref[j, 0:128, :], NT)
        dec = in_ref[j, 192:208, :].astype(f32)
        total = dec[0:1] + dec[1:2]
        state = r[:64] + r[64:] + total * state + in_ref[j, 128:192, :].astype(f32)


def row_sums(acc_ref, at):
    return jnp.sum(jnp.transpose(acc_ref[at * DH : (at + 1) * DH, :]), axis=0, keepdims=True)


def attn_kernel(idx_ref, q_ref, k0_ref, v0_ref, kv1_ref, kv2_ref, prev_ref, o_ref, sq_ref, s_ref, QB=256):
    rows = q_ref.shape[0]
    hb = q_ref.shape[1] // DH
    nb = rows // QB
    ctx = idx_ref[0]
    scale = math.log2(math.e) / math.sqrt(DH)

    bias1 = jnp.where(ctx >= 1, 0.0, 1e30).astype(f32)
    bias2 = jnp.where(ctx >= 2, 0.0, 1e30).astype(f32)
    ri = lax.broadcasted_iota(jnp.int32, (QB, QB), 0)
    ci = lax.broadcasted_iota(jnp.int32, (QB, QB), 1)
    far = ci > ri

    @pl.when(pl.program_id(0) == 0)
    def _():
        s_ref[...] = jnp.zeros_like(s_ref)

    pairs = [(h, b) for h in range(hb) for b in range(nb)]

    def scores(h, b):
        lanes = slice(h * DH, (h + 1) * DH)
        q = q_ref[b * QB : (b + 1) * QB, lanes]
        s2 = mm(q, kv2_ref[0, b * QB :, lanes], NT)
        s1 = mm(q, kv1_ref[0, :, lanes], NT)
        s0 = mm(q, k0_ref[: (b + 1) * QB, lanes], NT)
        return s2, s1, s0

    def weights(b, s2, s1, s0):
        st = jnp.where(far, s2[:, :QB] - bias2, s0[:, b * QB :])
        parts = [(st, None), (s1, bias1)]
        if b < nb - 1:
            parts.append((s2[:, QB:], bias2))
        if b > 0:
            parts.append((s0[:, : b * QB], None))
        top = None
        for part, bias in parts:
            most = jnp.max(part, axis=1, keepdims=True)
            most = most if bias is None else most - bias
            top = most if top is None else jnp.maximum(top, most)
        raised = [jnp.exp2((p - (top if x is None else top + x)) * scale) for p, x in parts]
        total = sum(jnp.sum(p, axis=1, keepdims=True) for p in raised)
        w2 = jnp.where(far, raised[0], 0.0).astype(bf16)
        w0 = jnp.where(far, 0.0, raised[0]).astype(bf16)
        if b < nb - 1:
            w2 = cat([w2, raised[2].astype(bf16)], 1)
        if b > 0:
            w0 = cat([raised[-1].astype(bf16), w0], 1)
        return w2, raised[1].astype(bf16), w0, total

    def finish(h, b, w2, w1, w0, total):
        lanes = slice(h * DH, (h + 1) * DH)
        out = mm(w1, kv1_ref[1, :, lanes]) + mm(w2, kv2_ref[1, b * QB :, lanes]) + mm(w0, v0_ref[: (b + 1) * QB, lanes])
        out = out * (1.0 / total)
        o_ref[b * QB : (b + 1) * QB, lanes] = out
        s_ref[b * QB : (b + 1) * QB, :] += out * out

    ready = scores(*pairs[0])
    waiting = None
    for i, (h, b) in enumerate(pairs):
        current = ready
        if i + 1 < len(pairs):
            ready = scores(*pairs[i + 1])
        made = weights(b, *current)
        if waiting is not None:
            finish(*waiting)
        waiting = (h, b, *made)
    finish(*waiting)

    @pl.when(pl.program_id(0) == pl.num_programs(0) - 1)
    def _():
        n = rows // DH
        sums = cat([row_sums(s_ref, i) for i in range(n)] + [jnp.zeros((n, DH), f32)], 0)
        sq_ref[...] = prev_ref[...] + sums


def apply_kernel(o_ref, y_ref, m_ref, t_ref, prev_ref, d_ref, sq_ref, s_ref):
    rows = o_ref.shape[0]
    hb = m_ref.shape[0]
    nc = rows // C

    @pl.when(pl.program_id(0) == 0)
    def _():
        s_ref[...] = jnp.zeros_like(s_ref)

    firsts = [cat([t_ref[2 * hh], t_ref[2 * hh + 1]], 0) for hh in range(hb)]
    pairs = [(hh, c) for c in range(1, nc) for hh in range(hb)]
    states = [
        m_ref[hh, c - 1][:, :DH].astype(f32) + mm(m_ref[hh, c - 1][:, DH:], firsts[hh], NT) for hh, c in pairs
    ]
    states = [split(x) for x in states]
    outs = {}
    for hh in range(hb):
        outs[hh, 0] = mm(tile(y_ref, hh, 0), firsts[hh], NT)
    for (hh, c), state in zip(pairs, states):
        y = tile(y_ref, hh, c)
        outs[hh, c] = mm(cat([y, y], 1), cat(state, 0))
    for (hh, c), moved in outs.items():
        out = tile(o_ref, hh, c) + moved
        at = slice(c * C, (c + 1) * C)
        d_ref[at, hh * DH : (hh + 1) * DH] = out
        s_ref[at, :] += out * out

    @pl.when(pl.program_id(0) == pl.num_programs(0) - 1)
    def _():
        n = rows // DH
        sums = cat([jnp.zeros((n, DH), f32)] + [row_sums(s_ref, i) for i in range(n)], 0)
        sq_ref[...] = prev_ref[...] + sums


def join_kernel(sq_ref, *refs):
    a_refs, (d_ref, ag_ref, dg_ref, o_ref) = refs[:-4], refs[-4:]
    n = sq_ref.shape[0] // 2
    scales = jnp.transpose(0.5 * lax.rsqrt(sq_ref[...] * (1.0 / WIDTH) + EPS))
    lane = lax.broadcasted_iota(jnp.int32, scales.shape, 1)
    i = pl.program_id(0)
    attn_scale = jnp.sum(jnp.where(lane == i, scales, 0.0), axis=1, keepdims=True)
    delta_scale = jnp.sum(jnp.where(lane == i + n, scales, 0.0), axis=1, keepdims=True)
    at = 0
    for a_ref in a_refs:
        lanes = slice(at, at + a_ref.shape[1])
        at += a_ref.shape[1]
        o_ref[:, lanes] = (
            ag_ref[:, lanes] * a_ref[...] * attn_scale + dg_ref[:, lanes] * d_ref[:, lanes] * delta_scale
        ).astype(bf16)


def params():
    return pltpu.CompilerParams(vmem_limit_bytes=60 * 2**20)


def cost(us):
    return pl.CostEstimate(flops=int(us * 1e9), bytes_accessed=0, transcendentals=0)


def on_device(aq, ak, av, dq, dk, dv, gate, beta, ag, dg):
    rows, width = aq.shape
    heads = gate.shape[1]
    nctx = lax.axis_size("ctx")
    nc = rows // C
    index = lax.axis_index("ctx").astype(jnp.int32).reshape(1)

    hop = [(i, i + 2) for i in range(nctx - 2)]
    swap = [(i, i + 1 - 2 * (i % 2)) for i in range(nctx)]
    odd = index[0] % 2 == 1

    def send(x, pairs):
        return lax.ppermute(x, "ctx", pairs)

    parts, at = [], 0
    for count in PARTS:
        parts.append((at * DH, count * DH))
        at += count
    own = [jnp.stack([x[:, at : at + size] for x in (ak, av)]) for at, size in parts]
    two = [send(x, hop) for x in own]

    gt = gate.T.reshape(heads, 1, rows)
    bt = beta.T.reshape(heads, 1, rows)

    def wide(hb):
        return pl.BlockSpec((rows, hb * DH), lambda h: (0, h))

    def lead(*shape):
        return pl.BlockSpec(shape, lambda h: (h,) + (0,) * (len(shape) - 1))

    def shaped(shape, dtype=f32):
        return jax.ShapeDtypeStruct(shape, dtype)

    hb = 4
    fixed, maps, logs, pay = pl.pallas_call(
        map_kernel,
        grid=(heads // hb,),
        in_specs=[wide(hb), wide(hb), lead(hb, 1, rows), lead(hb, 1, rows)],
        out_specs=[lead(hb, nc, C, 2 * DH), lead(hb, nc - 1, DH, 2 * DH), lead(hb, 2 * nc, 8, C), lead(2 * hb, PAY, DH)],
        out_shape=[
            shaped((heads, nc, C, 2 * DH), bf16),
            shaped((heads, nc - 1, DH, 2 * DH), bf16),
            shaped((heads, 2 * nc, 8, C)),
            shaped((nctx, PAY, DH), bf16),
        ],
        compiler_params=params(),
        cost_estimate=cost(COSTS[0]),
        name="delta_maps",
    )(dk, dv, gt, bt)

    got = lax.all_to_all(pay, "ctx", 0, 0, tiled=True)

    hb = 3
    local, effect = pl.pallas_call(
        out_kernel,
        grid=(heads // hb,),
        in_specs=[wide(hb), wide(hb), lead(hb, nc, C, 2 * DH), lead(hb, 2 * nc, 8, C)],
        out_specs=[wide(hb), wide(hb)],
        out_shape=[shaped((rows, width)), shaped((rows, width), bf16)],
        compiler_params=params(),
        cost_estimate=cost(COSTS[1]),
        name="delta_rows",
    )(dq, dk, fixed, logs)

    def before(i, token):
        two[i], token = lax.optimization_barrier((two[i], token))
        return send(jnp.where(odd, two[i], own[i]), swap), token

    one = [None] * len(parts)
    one[0], local = before(0, local)

    chain = pl.pallas_call(
        chain_kernel,
        out_shape=shaped((nctx, 64, DH), bf16),
        compiler_params=params(),
        cost_estimate=cost(COSTS[2]),
        name="delta_chain",
    )(got)

    whole = pl.BlockSpec((2 * rows // DH, DH), lambda h: (0, 0))
    hb = AH

    def attend(i, prev):
        steps = parts[i][1] // (hb * DH)
        first = parts[i][0] // (hb * DH)
        mine = pl.BlockSpec((rows, hb * DH), lambda h: (0, first + h))
        both = pl.BlockSpec((2, rows, hb * DH), lambda h: (0, 0, h))
        return pl.pallas_call(
            functools.partial(attn_kernel, QB=QB),
            grid=(steps,),
            in_specs=[pl.BlockSpec(memory_space=pltpu.SMEM), mine, mine, mine, both, both, whole],
            out_specs=[wide(hb), whole],
            out_shape=[shaped((rows, parts[i][1])), shaped((2 * rows // DH, DH))],
            scratch_shapes=[pltpu.VMEM((rows, DH), f32)],
            compiler_params=params(),
            cost_estimate=cost(COSTS[3]),
            name=f"window_attention_{i}",
        )(index, aq, ak, av, one[i], two[i], prev)

    squares = jnp.zeros((2 * rows // DH, DH), f32)
    squares, chain = lax.optimization_barrier((squares, chain))
    states = lax.all_to_all(chain, "ctx", 0, 0, tiled=True)
    attn = []
    out, squares = attend(0, squares)
    attn.append(out)
    one[1], squares = before(1, squares)

    hb = 2
    delta, squares = pl.pallas_call(
        apply_kernel,
        grid=(heads // hb,),
        in_specs=[wide(hb), wide(hb), lead(hb, nc - 1, DH, 2 * DH), lead(2 * hb, 64, DH), whole],
        out_specs=[wide(hb), whole],
        out_shape=[shaped((rows, width)), shaped((2 * rows // DH, DH))],
        scratch_shapes=[pltpu.VMEM((rows, DH), f32)],
        compiler_params=params(),
        cost_estimate=cost(COSTS[4]),
        name="delta_apply",
    )(local, effect, maps, states, squares)

    one[2], squares = before(2, squares)
    for i in range(1, len(parts)):
        out, squares = attend(i, squares)
        attn.append(out)
    squares = lax.psum(squares, "head")

    cols = pl.BlockSpec((DH, width), lambda i: (i, 0))
    gains = pl.BlockSpec((1, width), lambda i: (0, 0))
    return pl.pallas_call(
        join_kernel,
        grid=(rows // DH,),
        in_specs=[whole] + [pl.BlockSpec((DH, size), lambda i: (i, 0)) for _, size in parts] + [cols, gains, gains],
        out_specs=cols,
        out_shape=shaped((rows, width), bf16),
        compiler_params=params(),
        name="join",
    )(squares, *attn, delta, ag.reshape(1, width), dg.reshape(1, width))


def solution(mesh):
    shard = P("ctx", "head")
    return jax.shard_map(
        on_device,
        mesh=mesh,
        in_specs=(shard,) * 8 + (P("head"), P("head")),
        out_specs=shard,
        check_vma=False,
    )
```

```python
import functools
import math

import jax
import jax.numpy as jnp
from jax import lax
from jax.experimental import pallas as pl
from jax.experimental.pallas import tpu as pltpu
from jax.sharding import PartitionSpec as P

DH = 128
WIDTH = 6144
WINDOW = 1024
EPS = 1e-06
C = 128
PARTS = (6, 4, 2)
AH = 2
QB = 256
COSTS = (2, 8, 5, 1, 5)
PAY = 208
NEG = -1e30
f32 = jnp.float32
bf16 = jnp.bfloat16

NN = (((1,), (0,)), ((), ()))
NT = (((1,), (1,)), ((), ()))
TN = (((0,), (0,)), ((), ()))


def mm(a, b, dims=NN):
    return lax.dot_general(a, b, dims, preferred_element_type=f32)


def split(x):
    hi = x.astype(bf16)
    lo = (x - hi.astype(f32)).astype(bf16)
    return hi, lo


def cat(parts, axis):
    return jnp.concatenate(parts, axis=axis)


def dot3(a, b):
    (ah, al), (bh, bl) = a, b
    lhs = cat([ah, al], 1)
    rhs = cat([cat([bh, bl], 1), cat([bh, jnp.zeros_like(bl)], 1)], 0)
    r = mm(lhs, rhs)
    return r[:, :C] + r[:, C:]


def wide3(a, b):
    (ah, al), (bh, bl) = a, b
    return mm(cat([ah, al], 1), cat([bh, bh], 0)) + mm(ah, bl)


def block_rows(ref, c):
    return cat([ref[hh][:, c * C : (c + 1) * C] for hh in range(ref.shape[0])], 0)


def tile(ref, hh, c):
    return ref[c * C : (c + 1) * C, hh * DH : (hh + 1) * DH]


def iotas():
    ri = lax.broadcasted_iota(jnp.int32, (C, C), 0)
    ci = lax.broadcasted_iota(jnp.int32, (C, C), 1)
    return ri, ci


def pair_list(hb, nc):
    return [(hh, c) for hh in range(hb) for c in range(nc)]


def log_sums(g_ref, pairs, ri, ci):
    triu = jnp.where(ri <= ci, 1.0, 0.0).astype(f32)
    rows = cat([g_ref[hh][:, c * C : (c + 1) * C] for hh, c in pairs], 0)
    return lax.dot_general(
        jnp.log(rows), triu, NN, precision=lax.Precision.HIGHEST, preferred_element_type=f32
    )


def map_kernel(k_ref, v_ref, g_ref, b_ref, uw_ref, s_ref, l_ref, pay_ref):
    rows = k_ref.shape[0]
    hb = g_ref.shape[0]
    nc = rows // C
    units = range(hb * nc)
    pairs = pair_list(hb, nc)
    ri, ci = iotas()
    eye = ri == ci
    xor = jnp.where(ri > ci, ri ^ ci, 0)
    identity = jnp.where(eye, 1.0, 0.0).astype(f32)

    logs = log_sums(g_ref, pairs, ri, ci)
    beta = cat([b_ref[hh][:, c * C : (c + 1) * C] for hh, c in pairs], 0)
    keys = [tile(k_ref, hh, c) for hh, c in pairs]
    grams = [mm(k, k, NT) for k in keys]
    diag = cat([jnp.sum(jnp.where(eye, g, 0.0), axis=0, keepdims=True) for g in grams], 0)
    key_scale = lax.rsqrt(diag * (1.0 / DH) + EPS) * (1.0 / math.sqrt(DH))
    growth = jnp.exp(logs)
    last = logs[:, C - 1 : C]
    decay = jnp.exp(last)
    tail = jnp.exp(last - logs) * key_scale
    bs = beta * key_scale
    logs_c, tail_c, bs_c, beta_c, bgs_c = (
        jnp.transpose(x) for x in (logs, tail, bs, beta, bs * growth)
    )
    for u, (hh, c) in enumerate(pairs):
        l_ref[hh, c] = jnp.broadcast_to(logs[u : u + 1], (8, C))
        l_ref[hh, nc + c] = jnp.broadcast_to(key_scale[u : u + 1], (8, C))

    negs, invs = [], []
    for u in units:
        col = slice(u, u + 1)
        ratio = jnp.exp(jnp.where(ri > ci, logs_c[:, col] - logs[col, :], NEG)) * key_scale[col, :]
        neg = grams[u] * ratio * (-bs_c[:, col])
        negs.append(split(neg))
        invs.append(identity + jnp.where(xor == 1, neg, 0.0))
    for level in range(1, C.bit_length() - 1):
        mask = (xor >> level) == 1
        parts = [split(t) for t in invs]
        left = [dot3(parts[u], negs[u]) for u in units]
        both = [dot3(split(left[u]), parts[u]) for u in units]
        invs = [invs[u] + jnp.where(mask, both[u], 0.0) for u in units]
    invs = [split(t) for t in invs]

    right = []
    for u, (hh, c) in enumerate(pairs):
        col = slice(u, u + 1)
        v = tile(v_ref, hh, c).astype(f32) * beta_c[:, col]
        k = keys[u].astype(f32) * bgs_c[:, col]
        right.append(split(cat([v, k], 1)))
    fixed = [wide3(invs[u], right[u]) for u in units]
    for u, (hh, c) in enumerate(pairs):
        uw_ref[hh, c] = fixed[u].astype(bf16)
    turned = [jnp.transpose(k) for k in keys]
    ends = [split(fixed[u] * tail_c[:, u : u + 1]) for u in units]
    maps = [mm(cat([turned[u], turned[u]], 1), cat(ends[u], 0)) for u in units]
    zero = jnp.zeros((C, DH), f32)
    start = cat([zero, identity], 1)

    states = []
    for hh in range(hb):
        u = hh * nc
        m = maps[u]
        states.append(cat([m[:, :DH], decay[u : u + 1, :] * identity - m[:, DH:]], 1))
    for c in range(1, nc):
        parts = [split(s) for s in states]
        for hh in range(hb):
            s_ref[hh, c - 1] = states[hh].astype(bf16)
        moved = [wide3(split(maps[hh * nc + c][:, DH:]), parts[hh]) for hh in range(hb)]
        for hh in range(hb):
            u = hh * nc + c
            offset = cat([maps[u][:, :DH], zero], 1)
            states[hh] = decay[u : u + 1, :] * states[hh] + (offset - moved[hh])

    row16 = lax.broadcasted_iota(jnp.int32, (16, DH), 0)
    for hh in range(hb):
        total = decay[hh * nc : hh * nc + 1, :]
        for c in range(1, nc):
            total = total * decay[hh * nc + c : hh * nc + c + 1, :]
        linear = (states[hh][:, DH:] - total * identity).astype(bf16)
        offset = jnp.transpose(states[hh][:, :DH]).astype(bf16)
        wide = jnp.broadcast_to(total, (16, DH))
        th = wide.astype(bf16).astype(f32)
        decays = jnp.where(row16 == 0, th, jnp.where(row16 == 1, wide - th, 0.0)).astype(bf16)
        for half in range(2):
            pay_ref[2 * hh + half, 0:128, :] = linear
            pay_ref[2 * hh + half, 128:192, :] = offset[half * 64 : (half + 1) * 64]
            pay_ref[2 * hh + half, 192:208, :] = decays


def out_kernel(q_ref, k_ref, uw_ref, l_ref, o_ref, y_ref):
    rows = q_ref.shape[0]
    hb = uw_ref.shape[0]
    nc = rows // C
    pairs = pair_list(hb, nc)
    ri, ci = iotas()
    lower = ri >= ci
    raw = [mm(tile(q_ref, hh, c), tile(k_ref, hh, c), NT) for hh, c in pairs]
    inner, growth = [], []
    for u, (hh, c) in enumerate(pairs):
        log_row, key_scale = l_ref[hh, c][0:1], l_ref[hh, nc + c][0:1]
        logs_c = jnp.transpose(l_ref[hh, c])[:, 0:1]
        mh, ml = split(raw[u] * (jnp.exp(jnp.where(lower, logs_c - log_row, NEG)) * key_scale))
        uw = uw_ref[hh, c]
        inner.append(mm(cat([mh, ml], 1), cat([uw, uw], 0)))
        growth.append(jnp.exp(logs_c))
    for u, (hh, c) in enumerate(pairs):
        qf = tile(q_ref, hh, c).astype(f32)
        scale = lax.rsqrt(jnp.mean(qf * qf, axis=1, keepdims=True) + EPS) * (1.0 / math.sqrt(DH))
        at = (slice(c * C, (c + 1) * C), slice(hh * DH, (hh + 1) * DH))
        o_ref[at] = inner[u][:, :DH] * scale
        y_ref[at] = ((growth[u] * qf - inner[u][:, DH:]) * scale).astype(bf16)


def chain_kernel(in_ref, out_ref):
    n = in_ref.shape[0]
    state = jnp.zeros((64, DH), f32)
    for j in range(n):
        out_ref[j] = state.astype(out_ref.dtype)
        if j == n - 1:
            break
        sh, sl = split(state)
        r = mm(cat([sh, sl], 0), in_ref[j, 0:128, :], NT)
        dec = in_ref[j, 192:208, :].astype(f32)
        total = dec[0:1] + dec[1:2]
        state = r[:64] + r[64:] + total * state + in_ref[j, 128:192, :].astype(f32)


def row_sums(acc_ref, at):
    return jnp.sum(jnp.transpose(acc_ref[at * DH : (at + 1) * DH, :]), axis=0, keepdims=True)


def attn_kernel(idx_ref, q_ref, k0_ref, v0_ref, kv1_ref, kv2_ref, prev_ref, o_ref, sq_ref, s_ref, QB=256):
    rows = q_ref.shape[0]
    hb = q_ref.shape[1] // DH
    nb = rows // QB
    ctx = idx_ref[0]
    scale = math.log2(math.e) / math.sqrt(DH)

    bias1 = jnp.where(ctx >= 1, 0.0, 1e30).astype(f32)
    bias2 = jnp.where(ctx >= 2, 0.0, 1e30).astype(f32)
    ri = lax.broadcasted_iota(jnp.int32, (QB, QB), 0)
    ci = lax.broadcasted_iota(jnp.int32, (QB, QB), 1)
    far = ci > ri

    @pl.when(pl.program_id(0) == 0)
    def _():
        s_ref[...] = jnp.zeros_like(s_ref)

    pairs = [(h, b) for h in range(hb) for b in range(nb)]

    def scores(h, b):
        lanes = slice(h * DH, (h + 1) * DH)
        q = q_ref[b * QB : (b + 1) * QB, lanes]
        s2 = mm(q, kv2_ref[0, b * QB :, lanes], NT)
        s1 = mm(q, kv1_ref[0, :, lanes], NT)
        s0 = mm(q, k0_ref[: (b + 1) * QB, lanes], NT)
        return s2, s1, s0

    def weights(b, s2, s1, s0):
        st = jnp.where(far, s2[:, :QB] - bias2, s0[:, b * QB :])
        parts = [(st, None), (s1, bias1)]
        if b < nb - 1:
            parts.append((s2[:, QB:], bias2))
        if b > 0:
            parts.append((s0[:, : b * QB], None))
        top = None
        for part, bias in parts:
            most = jnp.max(part, axis=1, keepdims=True)
            most = most if bias is None else most - bias
            top = most if top is None else jnp.maximum(top, most)
        raised = [jnp.exp2((p - (top if x is None else top + x)) * scale) for p, x in parts]
        total = sum(jnp.sum(p, axis=1, keepdims=True) for p in raised)
        w2 = jnp.where(far, raised[0], 0.0).astype(bf16)
        w0 = jnp.where(far, 0.0, raised[0]).astype(bf16)
        if b < nb - 1:
            w2 = cat([w2, raised[2].astype(bf16)], 1)
        if b > 0:
            w0 = cat([raised[-1].astype(bf16), w0], 1)
        return w2, raised[1].astype(bf16), w0, total

    def finish(h, b, w2, w1, w0, total):
        lanes = slice(h * DH, (h + 1) * DH)
        out = mm(w1, kv1_ref[1, :, lanes]) + mm(w2, kv2_ref[1, b * QB :, lanes]) + mm(w0, v0_ref[: (b + 1) * QB, lanes])
        out = out * (1.0 / total)
        o_ref[b * QB : (b + 1) * QB, lanes] = out
        s_ref[b * QB : (b + 1) * QB, :] += out * out

    ready = scores(*pairs[0])
    waiting = None
    for i, (h, b) in enumerate(pairs):
        current = ready
        if i + 1 < len(pairs):
            ready = scores(*pairs[i + 1])
        made = weights(b, *current)
        if waiting is not None:
            finish(*waiting)
        waiting = (h, b, *made)
    finish(*waiting)

    @pl.when(pl.program_id(0) == pl.num_programs(0) - 1)
    def _():
        n = rows // DH
        sums = cat([row_sums(s_ref, i) for i in range(n)] + [jnp.zeros((n, DH), f32)], 0)
        sq_ref[...] = prev_ref[...] + sums


def apply_kernel(o_ref, y_ref, m_ref, t_ref, prev_ref, d_ref, sq_ref, s_ref):
    rows = o_ref.shape[0]
    hb = m_ref.shape[0]
    nc = rows // C

    @pl.when(pl.program_id(0) == 0)
    def _():
        s_ref[...] = jnp.zeros_like(s_ref)

    firsts = [cat([t_ref[2 * hh], t_ref[2 * hh + 1]], 0) for hh in range(hb)]
    pairs = [(hh, c) for c in range(1, nc) for hh in range(hb)]
    states = [
        m_ref[hh, c - 1][:, :DH].astype(f32) + mm(m_ref[hh, c - 1][:, DH:], firsts[hh], NT) for hh, c in pairs
    ]
    states = [split(x) for x in states]
    outs = {}
    for hh in range(hb):
        outs[hh, 0] = mm(tile(y_ref, hh, 0), firsts[hh], NT)
    for (hh, c), state in zip(pairs, states):
        y = tile(y_ref, hh, c)
        outs[hh, c] = mm(cat([y, y], 1), cat(state, 0))
    for (hh, c), moved in outs.items():
        out = tile(o_ref, hh, c) + moved
        at = slice(c * C, (c + 1) * C)
        d_ref[at, hh * DH : (hh + 1) * DH] = out
        s_ref[at, :] += out * out

    @pl.when(pl.program_id(0) == pl.num_programs(0) - 1)
    def _():
        n = rows // DH
        sums = cat([jnp.zeros((n, DH), f32)] + [row_sums(s_ref, i) for i in range(n)], 0)
        sq_ref[...] = prev_ref[...] + sums


def join_kernel(sq_ref, *refs):
    a_refs, (d_ref, ag_ref, dg_ref, o_ref) = refs[:-4], refs[-4:]
    n = sq_ref.shape[0] // 2
    scales = jnp.transpose(0.5 * lax.rsqrt(sq_ref[...] * (1.0 / WIDTH) + EPS))
    lane = lax.broadcasted_iota(jnp.int32, scales.shape, 1)
    i = pl.program_id(0)
    attn_scale = jnp.sum(jnp.where(lane == i, scales, 0.0), axis=1, keepdims=True)
    delta_scale = jnp.sum(jnp.where(lane == i + n, scales, 0.0), axis=1, keepdims=True)
    at = 0
    for a_ref in a_refs:
        lanes = slice(at, at + a_ref.shape[1])
        at += a_ref.shape[1]
        o_ref[:, lanes] = (
            ag_ref[:, lanes] * a_ref[...] * attn_scale + dg_ref[:, lanes] * d_ref[:, lanes] * delta_scale
        ).astype(bf16)


def params():
    return pltpu.CompilerParams(vmem_limit_bytes=60 * 2**20)


def cost(us):
    return pl.CostEstimate(flops=int(us * 1e9), bytes_accessed=0, transcendentals=0)


def on_device(aq, ak, av, dq, dk, dv, gate, beta, ag, dg):
    rows, width = aq.shape
    heads = gate.shape[1]
    nctx = lax.axis_size("ctx")
    nc = rows // C
    index = lax.axis_index("ctx").astype(jnp.int32).reshape(1)

    hop = [(i, i + 2) for i in range(nctx - 2)]
    swap = [(i, i + 1 - 2 * (i % 2)) for i in range(nctx)]
    odd = index[0] % 2 == 1

    def send(x, pairs):
        return lax.ppermute(x, "ctx", pairs)

    parts, at = [], 0
    for count in PARTS:
        parts.append((at * DH, count * DH))
        at += count
    own = [jnp.stack([x[:, at : at + size] for x in (ak, av)]) for at, size in parts]
    two = [send(x, hop) for x in own]

    gt = gate.T.reshape(heads, 1, rows)
    bt = beta.T.reshape(heads, 1, rows)

    def wide(hb):
        return pl.BlockSpec((rows, hb * DH), lambda h: (0, h))

    def lead(*shape):
        return pl.BlockSpec(shape, lambda h: (h,) + (0,) * (len(shape) - 1))

    def shaped(shape, dtype=f32):
        return jax.ShapeDtypeStruct(shape, dtype)

    hb = 4
    fixed, maps, logs, pay = pl.pallas_call(
        map_kernel,
        grid=(heads // hb,),
        in_specs=[wide(hb), wide(hb), lead(hb, 1, rows), lead(hb, 1, rows)],
        out_specs=[lead(hb, nc, C, 2 * DH), lead(hb, nc - 1, DH, 2 * DH), lead(hb, 2 * nc, 8, C), lead(2 * hb, PAY, DH)],
        out_shape=[
            shaped((heads, nc, C, 2 * DH), bf16),
            shaped((heads, nc - 1, DH, 2 * DH), bf16),
            shaped((heads, 2 * nc, 8, C)),
            shaped((nctx, PAY, DH), bf16),
        ],
        compiler_params=params(),
        cost_estimate=cost(COSTS[0]),
        name="delta_maps",
    )(dk, dv, gt, bt)

    got = lax.all_to_all(pay, "ctx", 0, 0, tiled=True)

    hb = 3
    local, effect = pl.pallas_call(
        out_kernel,
        grid=(heads // hb,),
        in_specs=[wide(hb), wide(hb), lead(hb, nc, C, 2 * DH), lead(hb, 2 * nc, 8, C)],
        out_specs=[wide(hb), wide(hb)],
        out_shape=[shaped((rows, width)), shaped((rows, width), bf16)],
        compiler_params=params(),
        cost_estimate=cost(COSTS[1]),
        name="delta_rows",
    )(dq, dk, fixed, logs)

    def before(i, token):
        two[i], token = lax.optimization_barrier((two[i], token))
        return send(jnp.where(odd, two[i], own[i]), swap), token

    one = [None] * len(parts)
    one[0], local = before(0, local)

    chain = pl.pallas_call(
        chain_kernel,
        out_shape=shaped((nctx, 64, DH), bf16),
        compiler_params=params(),
        cost_estimate=cost(COSTS[2]),
        name="delta_chain",
    )(got)

    whole = pl.BlockSpec((2 * rows // DH, DH), lambda h: (0, 0))
    hb = AH

    def attend(i, prev):
        steps = parts[i][1] // (hb * DH)
        first = parts[i][0] // (hb * DH)
        mine = pl.BlockSpec((rows, hb * DH), lambda h: (0, first + h))
        both = pl.BlockSpec((2, rows, hb * DH), lambda h: (0, 0, h))
        return pl.pallas_call(
            functools.partial(attn_kernel, QB=QB),
            grid=(steps,),
            in_specs=[pl.BlockSpec(memory_space=pltpu.SMEM), mine, mine, mine, both, both, whole],
            out_specs=[wide(hb), whole],
            out_shape=[shaped((rows, parts[i][1])), shaped((2 * rows // DH, DH))],
            scratch_shapes=[pltpu.VMEM((rows, DH), f32)],
            compiler_params=params(),
            cost_estimate=cost(COSTS[3]),
            name=f"window_attention_{i}",
        )(index, aq, ak, av, one[i], two[i], prev)

    squares = jnp.zeros((2 * rows // DH, DH), f32)
    squares, chain = lax.optimization_barrier((squares, chain))
    states = lax.all_to_all(chain, "ctx", 0, 0, tiled=True)
    attn = []
    one[1], squares = before(1, squares)
    out, squares = attend(0, squares)
    attn.append(out)
    one[2], squares = before(2, squares)
    out, squares = attend(1, squares)
    attn.append(out)

    hb = 2
    delta, squares = pl.pallas_call(
        apply_kernel,
        grid=(heads // hb,),
        in_specs=[wide(hb), wide(hb), lead(hb, nc - 1, DH, 2 * DH), lead(2 * hb, 64, DH), whole],
        out_specs=[wide(hb), whole],
        out_shape=[shaped((rows, width)), shaped((2 * rows // DH, DH))],
        scratch_shapes=[pltpu.VMEM((rows, DH), f32)],
        compiler_params=params(),
        cost_estimate=cost(COSTS[4]),
        name="delta_apply",
    )(local, effect, maps, states, squares)

    out, squares = attend(2, squares)
    attn.append(out)
    squares = lax.psum(squares, "head")

    cols = pl.BlockSpec((DH, width), lambda i: (i, 0))
    gains = pl.BlockSpec((1, width), lambda i: (0, 0))
    return pl.pallas_call(
        join_kernel,
        grid=(rows // DH,),
        in_specs=[whole] + [pl.BlockSpec((DH, size), lambda i: (i, 0)) for _, size in parts] + [cols, gains, gains],
        out_specs=cols,
        out_shape=shaped((rows, width), bf16),
        compiler_params=params(),
        name="join",
    )(squares, *attn, delta, ag.reshape(1, width), dg.reshape(1, width))


def solution(mesh):
    shard = P("ctx", "head")
    return jax.shard_map(
        on_device,
        mesh=mesh,
        in_specs=(shard,) * 8 + (P("head"), P("head")),
        out_specs=shard,
        check_vma=False,
    )
```

```python
import functools
import math

import jax
import jax.numpy as jnp
from jax import lax
from jax.experimental import pallas as pl
from jax.experimental.pallas import tpu as pltpu
from jax.sharding import PartitionSpec as P

DH = 128
WIDTH = 6144
WINDOW = 1024
EPS = 1e-06
C = 128
PARTS = (6, 4, 2)
AH = 2
QB = 256
COSTS = (2, 8, 5, 1, 5)
PAY = 208
NEG = -1e30
f32 = jnp.float32
bf16 = jnp.bfloat16

NN = (((1,), (0,)), ((), ()))
NT = (((1,), (1,)), ((), ()))
TN = (((0,), (0,)), ((), ()))


def mm(a, b, dims=NN):
    return lax.dot_general(a, b, dims, preferred_element_type=f32)


def split(x):
    hi = x.astype(bf16)
    lo = (x - hi.astype(f32)).astype(bf16)
    return hi, lo


def cat(parts, axis):
    return jnp.concatenate(parts, axis=axis)


def dot3(a, b):
    (ah, al), (bh, bl) = a, b
    lhs = cat([ah, al], 1)
    rhs = cat([cat([bh, bl], 1), cat([bh, jnp.zeros_like(bl)], 1)], 0)
    r = mm(lhs, rhs)
    return r[:, :C] + r[:, C:]


def wide3(a, b):
    (ah, al), (bh, bl) = a, b
    return mm(cat([ah, al], 1), cat([bh, bh], 0)) + mm(ah, bl)


def block_rows(ref, c):
    return cat([ref[hh][:, c * C : (c + 1) * C] for hh in range(ref.shape[0])], 0)


def tile(ref, hh, c):
    return ref[c * C : (c + 1) * C, hh * DH : (hh + 1) * DH]


def iotas():
    ri = lax.broadcasted_iota(jnp.int32, (C, C), 0)
    ci = lax.broadcasted_iota(jnp.int32, (C, C), 1)
    return ri, ci


def pair_list(hb, nc):
    return [(hh, c) for hh in range(hb) for c in range(nc)]


def log_sums(g_ref, pairs, ri, ci):
    triu = jnp.where(ri <= ci, 1.0, 0.0).astype(f32)
    rows = cat([g_ref[hh][:, c * C : (c + 1) * C] for hh, c in pairs], 0)
    return lax.dot_general(
        jnp.log(rows), triu, NN, precision=lax.Precision.HIGHEST, preferred_element_type=f32
    )


def map_kernel(k_ref, v_ref, g_ref, b_ref, uw_ref, s_ref, l_ref, pay_ref):
    rows = k_ref.shape[0]
    hb = g_ref.shape[0]
    nc = rows // C
    units = range(hb * nc)
    pairs = pair_list(hb, nc)
    ri, ci = iotas()
    eye = ri == ci
    xor = jnp.where(ri > ci, ri ^ ci, 0)
    identity = jnp.where(eye, 1.0, 0.0).astype(f32)

    logs = log_sums(g_ref, pairs, ri, ci)
    beta = cat([b_ref[hh][:, c * C : (c + 1) * C] for hh, c in pairs], 0)
    keys = [tile(k_ref, hh, c) for hh, c in pairs]
    grams = [mm(k, k, NT) for k in keys]
    diag = cat([jnp.sum(jnp.where(eye, g, 0.0), axis=0, keepdims=True) for g in grams], 0)
    key_scale = lax.rsqrt(diag * (1.0 / DH) + EPS) * (1.0 / math.sqrt(DH))
    growth = jnp.exp(logs)
    last = logs[:, C - 1 : C]
    decay = jnp.exp(last)
    tail = jnp.exp(last - logs) * key_scale
    bs = beta * key_scale
    logs_c, tail_c, bs_c, beta_c, bgs_c = (
        jnp.transpose(x) for x in (logs, tail, bs, beta, bs * growth)
    )
    for u, (hh, c) in enumerate(pairs):
        l_ref[hh, c] = jnp.broadcast_to(logs[u : u + 1], (8, C))
        l_ref[hh, nc + c] = jnp.broadcast_to(key_scale[u : u + 1], (8, C))

    negs, invs = [], []
    for u in units:
        col = slice(u, u + 1)
        ratio = jnp.exp(jnp.where(ri > ci, logs_c[:, col] - logs[col, :], NEG)) * key_scale[col, :]
        neg = grams[u] * ratio * (-bs_c[:, col])
        negs.append(split(neg))
        invs.append(identity + jnp.where(xor == 1, neg, 0.0))
    for level in range(1, C.bit_length() - 1):
        mask = (xor >> level) == 1
        parts = [split(t) for t in invs]
        left = [dot3(parts[u], negs[u]) for u in units]
        both = [dot3(split(left[u]), parts[u]) for u in units]
        invs = [invs[u] + jnp.where(mask, both[u], 0.0) for u in units]
    invs = [split(t) for t in invs]

    right = []
    for u, (hh, c) in enumerate(pairs):
        col = slice(u, u + 1)
        v = tile(v_ref, hh, c).astype(f32) * beta_c[:, col]
        k = keys[u].astype(f32) * bgs_c[:, col]
        right.append(split(cat([v, k], 1)))
    fixed = [wide3(invs[u], right[u]) for u in units]
    for u, (hh, c) in enumerate(pairs):
        uw_ref[hh, c] = fixed[u].astype(bf16)
    turned = [jnp.transpose(k) for k in keys]
    ends = [split(fixed[u] * tail_c[:, u : u + 1]) for u in units]
    maps = [mm(cat([turned[u], turned[u]], 1), cat(ends[u], 0)) for u in units]
    zero = jnp.zeros((C, DH), f32)
    start = cat([zero, identity], 1)

    states = []
    for hh in range(hb):
        u = hh * nc
        m = maps[u]
        states.append(cat([m[:, :DH], decay[u : u + 1, :] * identity - m[:, DH:]], 1))
    for c in range(1, nc):
        parts = [split(s) for s in states]
        for hh in range(hb):
            s_ref[hh, c - 1] = states[hh].astype(bf16)
        moved = [wide3(split(maps[hh * nc + c][:, DH:]), parts[hh]) for hh in range(hb)]
        for hh in range(hb):
            u = hh * nc + c
            offset = cat([maps[u][:, :DH], zero], 1)
            states[hh] = decay[u : u + 1, :] * states[hh] + (offset - moved[hh])

    row16 = lax.broadcasted_iota(jnp.int32, (16, DH), 0)
    for hh in range(hb):
        total = decay[hh * nc : hh * nc + 1, :]
        for c in range(1, nc):
            total = total * decay[hh * nc + c : hh * nc + c + 1, :]
        linear = (states[hh][:, DH:] - total * identity).astype(bf16)
        offset = jnp.transpose(states[hh][:, :DH]).astype(bf16)
        wide = jnp.broadcast_to(total, (16, DH))
        th = wide.astype(bf16).astype(f32)
        decays = jnp.where(row16 == 0, th, jnp.where(row16 == 1, wide - th, 0.0)).astype(bf16)
        for half in range(2):
            pay_ref[2 * hh + half, 0:128, :] = linear
            pay_ref[2 * hh + half, 128:192, :] = offset[half * 64 : (half + 1) * 64]
            pay_ref[2 * hh + half, 192:208, :] = decays


def out_kernel(q_ref, k_ref, uw_ref, l_ref, o_ref, y_ref):
    rows = q_ref.shape[0]
    hb = uw_ref.shape[0]
    nc = rows // C
    pairs = pair_list(hb, nc)
    ri, ci = iotas()
    lower = ri >= ci
    raw = [mm(tile(q_ref, hh, c), tile(k_ref, hh, c), NT) for hh, c in pairs]
    inner, growth = [], []
    for u, (hh, c) in enumerate(pairs):
        log_row, key_scale = l_ref[hh, c][0:1], l_ref[hh, nc + c][0:1]
        logs_c = jnp.transpose(l_ref[hh, c])[:, 0:1]
        mh, ml = split(raw[u] * (jnp.exp(jnp.where(lower, logs_c - log_row, NEG)) * key_scale))
        uw = uw_ref[hh, c]
        inner.append(mm(cat([mh, ml], 1), cat([uw, uw], 0)))
        growth.append(jnp.exp(logs_c))
    for u, (hh, c) in enumerate(pairs):
        qf = tile(q_ref, hh, c).astype(f32)
        scale = lax.rsqrt(jnp.mean(qf * qf, axis=1, keepdims=True) + EPS) * (1.0 / math.sqrt(DH))
        at = (slice(c * C, (c + 1) * C), slice(hh * DH, (hh + 1) * DH))
        o_ref[at] = inner[u][:, :DH] * scale
        y_ref[at] = ((growth[u] * qf - inner[u][:, DH:]) * scale).astype(bf16)


def chain_kernel(in_ref, out_ref):
    n = in_ref.shape[0]
    state = jnp.zeros((64, DH), f32)
    for j in range(n):
        out_ref[j] = state.astype(out_ref.dtype)
        if j == n - 1:
            break
        sh, sl = split(state)
        r = mm(cat([sh, sl], 0), in_ref[j, 0:128, :], NT)
        dec = in_ref[j, 192:208, :].astype(f32)
        total = dec[0:1] + dec[1:2]
        state = r[:64] + r[64:] + total * state + in_ref[j, 128:192, :].astype(f32)


def row_sums(acc_ref, at):
    return jnp.sum(jnp.transpose(acc_ref[at * DH : (at + 1) * DH, :]), axis=0, keepdims=True)


def attn_kernel(idx_ref, q_ref, k0_ref, v0_ref, kv1_ref, kv2_ref, prev_ref, o_ref, sq_ref, s_ref, QB=256):
    rows = q_ref.shape[0]
    hb = q_ref.shape[1] // DH
    nb = rows // QB
    ctx = idx_ref[0]
    scale = math.log2(math.e) / math.sqrt(DH)

    bias1 = jnp.where(ctx >= 1, 0.0, 1e30).astype(f32)
    bias2 = jnp.where(ctx >= 2, 0.0, 1e30).astype(f32)
    ri = lax.broadcasted_iota(jnp.int32, (QB, QB), 0)
    ci = lax.broadcasted_iota(jnp.int32, (QB, QB), 1)
    far = ci > ri

    @pl.when(pl.program_id(0) == 0)
    def _():
        s_ref[...] = jnp.zeros_like(s_ref)

    pairs = [(h, b) for h in range(hb) for b in range(nb)]

    def scores(h, b):
        lanes = slice(h * DH, (h + 1) * DH)
        q = q_ref[b * QB : (b + 1) * QB, lanes]
        s2 = mm(q, kv2_ref[0, b * QB :, lanes], NT)
        s1 = mm(q, kv1_ref[0, :, lanes], NT)
        s0 = mm(q, k0_ref[: (b + 1) * QB, lanes], NT)
        return s2, s1, s0

    def weights(b, s2, s1, s0):
        st = jnp.where(far, s2[:, :QB] - bias2, s0[:, b * QB :])
        parts = [(st, None), (s1, bias1)]
        if b < nb - 1:
            parts.append((s2[:, QB:], bias2))
        if b > 0:
            parts.append((s0[:, : b * QB], None))
        top = None
        for part, bias in parts:
            most = jnp.max(part, axis=1, keepdims=True)
            most = most if bias is None else most - bias
            top = most if top is None else jnp.maximum(top, most)
        raised = [jnp.exp2((p - (top if x is None else top + x)) * scale) for p, x in parts]
        total = sum(jnp.sum(p, axis=1, keepdims=True) for p in raised)
        w2 = jnp.where(far, raised[0], 0.0).astype(bf16)
        w0 = jnp.where(far, 0.0, raised[0]).astype(bf16)
        if b < nb - 1:
            w2 = cat([w2, raised[2].astype(bf16)], 1)
        if b > 0:
            w0 = cat([raised[-1].astype(bf16), w0], 1)
        return w2, raised[1].astype(bf16), w0, total

    def finish(h, b, w2, w1, w0, total):
        lanes = slice(h * DH, (h + 1) * DH)
        out = mm(w1, kv1_ref[1, :, lanes]) + mm(w2, kv2_ref[1, b * QB :, lanes]) + mm(w0, v0_ref[: (b + 1) * QB, lanes])
        out = out * (1.0 / total)
        o_ref[b * QB : (b + 1) * QB, lanes] = out
        s_ref[b * QB : (b + 1) * QB, :] += out * out

    ready = scores(*pairs[0])
    waiting = None
    for i, (h, b) in enumerate(pairs):
        current = ready
        if i + 1 < len(pairs):
            ready = scores(*pairs[i + 1])
        made = weights(b, *current)
        if waiting is not None:
            finish(*waiting)
        waiting = (h, b, *made)
    finish(*waiting)

    @pl.when(pl.program_id(0) == pl.num_programs(0) - 1)
    def _():
        n = rows // DH
        sums = cat([row_sums(s_ref, i) for i in range(n)] + [jnp.zeros((n, DH), f32)], 0)
        sq_ref[...] = prev_ref[...] + sums


def apply_kernel(o_ref, y_ref, m_ref, t_ref, prev_ref, d_ref, sq_ref, s_ref):
    rows = o_ref.shape[0]
    hb = m_ref.shape[0]
    nc = rows // C

    @pl.when(pl.program_id(0) == 0)
    def _():
        s_ref[...] = jnp.zeros_like(s_ref)

    firsts = [cat([t_ref[2 * hh], t_ref[2 * hh + 1]], 0) for hh in range(hb)]
    pairs = [(hh, c) for c in range(1, nc) for hh in range(hb)]
    states = [
        m_ref[hh, c - 1][:, :DH].astype(f32) + mm(m_ref[hh, c - 1][:, DH:], firsts[hh], NT) for hh, c in pairs
    ]
    states = [split(x) for x in states]
    outs = {}
    for hh in range(hb):
        outs[hh, 0] = mm(tile(y_ref, hh, 0), firsts[hh], NT)
    for (hh, c), state in zip(pairs, states):
        y = tile(y_ref, hh, c)
        outs[hh, c] = mm(cat([y, y], 1), cat(state, 0))
    for (hh, c), moved in outs.items():
        out = tile(o_ref, hh, c) + moved
        at = slice(c * C, (c + 1) * C)
        d_ref[at, hh * DH : (hh + 1) * DH] = out
        s_ref[at, :] += out * out

    @pl.when(pl.program_id(0) == pl.num_programs(0) - 1)
    def _():
        n = rows // DH
        sums = cat([jnp.zeros((n, DH), f32)] + [row_sums(s_ref, i) for i in range(n)], 0)
        sq_ref[...] = prev_ref[...] + sums


def join_kernel(sq_ref, *refs):
    a_refs, (d_ref, ag_ref, dg_ref, o_ref) = refs[:-4], refs[-4:]
    n = sq_ref.shape[0] // 2
    scales = jnp.transpose(0.5 * lax.rsqrt(sq_ref[...] * (1.0 / WIDTH) + EPS))
    lane = lax.broadcasted_iota(jnp.int32, scales.shape, 1)
    i = pl.program_id(0)
    per = o_ref.shape[0] // DH

    def column(first):
        parts = [jnp.sum(jnp.where(lane == first + k, scales, 0.0), axis=1, keepdims=True) for k in range(per)]
        return cat(parts, 0)

    attn_scale, delta_scale = column(i * per), column(i * per + n)
    at = 0
    for a_ref in a_refs:
        lanes = slice(at, at + a_ref.shape[1])
        at += a_ref.shape[1]
        o_ref[:, lanes] = (
            ag_ref[:, lanes] * a_ref[...] * attn_scale + dg_ref[:, lanes] * d_ref[:, lanes] * delta_scale
        ).astype(bf16)


def params():
    return pltpu.CompilerParams(vmem_limit_bytes=60 * 2**20)


def cost(us):
    return pl.CostEstimate(flops=int(us * 1e9), bytes_accessed=0, transcendentals=0)


def on_device(aq, ak, av, dq, dk, dv, gate, beta, ag, dg):
    rows, width = aq.shape
    heads = gate.shape[1]
    nctx = lax.axis_size("ctx")
    nc = rows // C
    index = lax.axis_index("ctx").astype(jnp.int32).reshape(1)

    hop = [(i, i + 2) for i in range(nctx - 2)]
    swap = [(i, i + 1 - 2 * (i % 2)) for i in range(nctx)]
    odd = index[0] % 2 == 1

    def send(x, pairs):
        return lax.ppermute(x, "ctx", pairs)

    parts, at = [], 0
    for count in PARTS:
        parts.append((at * DH, count * DH))
        at += count
    own = [jnp.stack([x[:, at : at + size] for x in (ak, av)]) for at, size in parts]
    two = [send(x, hop) for x in own]

    gt = gate.T.reshape(heads, 1, rows)
    bt = beta.T.reshape(heads, 1, rows)

    def wide(hb):
        return pl.BlockSpec((rows, hb * DH), lambda h: (0, h))

    def lead(*shape):
        return pl.BlockSpec(shape, lambda h: (h,) + (0,) * (len(shape) - 1))

    def shaped(shape, dtype=f32):
        return jax.ShapeDtypeStruct(shape, dtype)

    hb = 4
    fixed, maps, logs, pay = pl.pallas_call(
        map_kernel,
        grid=(heads // hb,),
        in_specs=[wide(hb), wide(hb), lead(hb, 1, rows), lead(hb, 1, rows)],
        out_specs=[lead(hb, nc, C, 2 * DH), lead(hb, nc - 1, DH, 2 * DH), lead(hb, 2 * nc, 8, C), lead(2 * hb, PAY, DH)],
        out_shape=[
            shaped((heads, nc, C, 2 * DH), bf16),
            shaped((heads, nc - 1, DH, 2 * DH), bf16),
            shaped((heads, 2 * nc, 8, C)),
            shaped((nctx, PAY, DH), bf16),
        ],
        compiler_params=params(),
        cost_estimate=cost(COSTS[0]),
        name="delta_maps",
    )(dk, dv, gt, bt)

    got = lax.all_to_all(pay, "ctx", 0, 0, tiled=True)

    hb = 3
    local, effect = pl.pallas_call(
        out_kernel,
        grid=(heads // hb,),
        in_specs=[wide(hb), wide(hb), lead(hb, nc, C, 2 * DH), lead(hb, 2 * nc, 8, C)],
        out_specs=[wide(hb), wide(hb)],
        out_shape=[shaped((rows, width)), shaped((rows, width), bf16)],
        compiler_params=params(),
        cost_estimate=cost(COSTS[1]),
        name="delta_rows",
    )(dq, dk, fixed, logs)

    def before(i, token):
        two[i], token = lax.optimization_barrier((two[i], token))
        return send(jnp.where(odd, two[i], own[i]), swap), token

    one = [None] * len(parts)
    one[0], local = before(0, local)

    chain = pl.pallas_call(
        chain_kernel,
        out_shape=shaped((nctx, 64, DH), bf16),
        compiler_params=params(),
        cost_estimate=cost(COSTS[2]),
        name="delta_chain",
    )(got)

    whole = pl.BlockSpec((2 * rows // DH, DH), lambda h: (0, 0))
    hb = AH

    def attend(i, prev):
        steps = parts[i][1] // (hb * DH)
        first = parts[i][0] // (hb * DH)
        mine = pl.BlockSpec((rows, hb * DH), lambda h: (0, first + h))
        both = pl.BlockSpec((2, rows, hb * DH), lambda h: (0, 0, h))
        return pl.pallas_call(
            functools.partial(attn_kernel, QB=QB),
            grid=(steps,),
            in_specs=[pl.BlockSpec(memory_space=pltpu.SMEM), mine, mine, mine, both, both, whole],
            out_specs=[wide(hb), whole],
            out_shape=[shaped((rows, parts[i][1])), shaped((2 * rows // DH, DH))],
            scratch_shapes=[pltpu.VMEM((rows, DH), f32)],
            compiler_params=params(),
            cost_estimate=cost(COSTS[3]),
            name=f"window_attention_{i}",
        )(index, aq, ak, av, one[i], two[i], prev)

    squares = jnp.zeros((2 * rows // DH, DH), f32)
    squares, chain = lax.optimization_barrier((squares, chain))
    states = lax.all_to_all(chain, "ctx", 0, 0, tiled=True)
    attn = []
    one[1], squares = before(1, squares)
    out, squares = attend(0, squares)
    attn.append(out)
    one[2], squares = before(2, squares)
    out, squares = attend(1, squares)
    attn.append(out)

    hb = 2
    delta, squares = pl.pallas_call(
        apply_kernel,
        grid=(heads // hb,),
        in_specs=[wide(hb), wide(hb), lead(hb, nc - 1, DH, 2 * DH), lead(2 * hb, 64, DH), whole],
        out_specs=[wide(hb), whole],
        out_shape=[shaped((rows, width)), shaped((2 * rows // DH, DH))],
        scratch_shapes=[pltpu.VMEM((rows, DH), f32)],
        compiler_params=params(),
        cost_estimate=cost(COSTS[4]),
        name="delta_apply",
    )(local, effect, maps, states, squares)

    out, squares = attend(2, squares)
    attn.append(out)
    squares = lax.psum(squares, "head")

    block = 2 * DH
    cols = pl.BlockSpec((block, width), lambda i: (i, 0))
    gains = pl.BlockSpec((1, width), lambda i: (0, 0))
    return pl.pallas_call(
        join_kernel,
        grid=(rows // block,),
        in_specs=[whole] + [pl.BlockSpec((block, size), lambda i: (i, 0)) for _, size in parts] + [cols, gains, gains],
        out_specs=cols,
        out_shape=shaped((rows, width), bf16),
        compiler_params=params(),
        name="join",
    )(squares, *attn, delta, ag.reshape(1, width), dg.reshape(1, width))


def solution(mesh):
    shard = P("ctx", "head")
    return jax.shard_map(
        on_device,
        mesh=mesh,
        in_specs=(shard,) * 8 + (P("head"), P("head")),
        out_specs=shard,
        check_vma=False,
    )
```
